32 devices in a mesh: train: 2 (over y), replica: 4 (over x, core), ep: 4 (over z).
Axes of the slice: x: 2, y: 2, z: 4, core: 2. Of those that a mesh axis runs over, the one named last changes fastest.
Arguments:
- master: float32 [8, 2048, 7168], P('ep', 'replica', 'train'), may hold values from -6 to 6
- gradient: bfloat16 [8, 2048, 7168], P('ep', 'replica', 'train'), may hold values from -1000 to 1000
- second: float32 [8, 2048, 7168], P('ep', 'replica', 'train'), may hold values from 0.1 to 2
- placement: int32 [4, 8], replicated, may hold values from 0 to 3, as said below
Outputs:
- master_new: float32 [8, 2048, 7168], P('ep', 'replica', 'train')
- second_new: float32 [8, 2048, 7168], P('ep', 'replica', 'train')
- quantized: bfloat16 [4, 4, 2, 2048, 7168], P('replica', 'ep', None, None, 'train')
- scales: float32 [4, 4, 2, 16, 56], P('replica', 'ep', None, None, 'train')
The draws below stay inside these ranges and needn't reach their ends.
Inputs may be any that keep to these rules, and one draw needn't show every extreme that they name: `placement`: in each row every ep index is named by exactly 2 experts.
All inputs are finite; a program needn't handle non-finite values. Where the reference program divides by a largest or mean magnitude, that divisor is 1e-20 or more.
Results may differ from the reference program's by a relative error of at most 0.006.
Values may be sent and summed in bfloat16 or wider, within the bound.
A program may use at most 320 MiB of HBM per device.

```python
import math
import jax
import jax.numpy as jnp
from jax import lax

D = 7168
FF = 2048
EXP_DEV = 2
BLOCK = 128
EXPERTS = 8
N_REPLICA = 4
N_EP = 4


def draw_gradient(key, part):
    key = jax.random.fold_in(key, 11)
    first_key, second_key, third_key = jax.random.split(key, 3)
    base = jnp.clip(jax.random.normal(first_key, (EXPERTS, FF, D), jnp.float32), -6.0, 6.0)
    power = 0.5
    along_experts = jnp.arange(EXPERTS, dtype=jnp.float32)[:, None, None] / EXPERTS
    along_rows = jnp.arange(FF, dtype=jnp.float32)[None, :, None] / FF
    along_columns = jnp.arange(D, dtype=jnp.float32)[None, None, :] / D
    trend = jnp.exp(power * math.log(3.0) * (along_experts + along_rows + along_columns))
    row_scale = jnp.exp(jax.random.uniform(second_key, (EXPERTS, FF, 1), jnp.float32, 0.0, math.log(3.2)))
    column_scale = jnp.exp(jax.random.uniform(third_key, (EXPERTS, 1, D), jnp.float32, 0.0, math.log(3.2)))
    return (2.0 * base * trend * row_scale * column_scale).astype(jnp.bfloat16)


def draw_placement(key, part):
    key = jax.random.fold_in(key, 23)
    replica_keys = jax.random.split(key, N_REPLICA)
    orders = jax.vmap(lambda single: jax.random.permutation(single, EXPERTS))(replica_keys)
    return (orders // EXP_DEV).astype(jnp.int32)


def block_scale(own_key, shape, cuts, least, high):
    factor_of, own = 1.0, jax.random.fold_in(own_key, 6)
    for dim, parts in cuts:
        draws = jnp.exp(jax.random.uniform(jax.random.fold_in(own, dim), (parts,), jnp.float32, least / len(cuts), high / len(cuts)))
        factor_of = factor_of * jnp.repeat(draws, shape[dim] // parts).reshape([-1 if axis == dim else 1 for axis in range(len(shape))])
    return factor_of


def centred(rng, extent, spread, bound, cuts=(), kind=jnp.bfloat16):
    loudness = block_scale(rng, extent, cuts, -0.22, 0.18) if cuts else 1.0
    entries = jax.random.normal(rng, extent, jnp.float32) * spread * loudness
    return jnp.minimum(jnp.maximum(entries, -bound), bound).astype(kind)


def setup_inputs(seed: int = 0) -> dict:
    key_list = jax.random.split(jax.random.key(seed), 5)
    return {
        "master": centred(key_list[0], (EXPERTS, FF, D), 1.0, 6.0, ((0, 4), (1, 4), (2, 2)), jnp.float32),
        "gradient": draw_gradient(jax.random.fold_in(key_list[4], 71), 0),
        "second": jnp.clip(jnp.exp(math.log(2.0) - 2.9957323 * jax.random.uniform(key_list[2], (EXPERTS, FF, D), jnp.float32) ** block_scale(key_list[2], (EXPERTS, FF, D), ((0, 4), (1, 4), (2, 2)), -0.2, 0.2)), 0.1, 2.0),
        "placement": draw_placement(jax.random.fold_in(key_list[4], 71), 0),
    }


decay_rate = 0.95
step_size = 0.3

def block_quantize(values):
    full_shape = values.shape
    blocks = values.astype(jnp.float32).reshape(full_shape[:-2] + (full_shape[-2] // BLOCK, BLOCK, full_shape[-1] // BLOCK, BLOCK))
    largest = lax.optimization_barrier(jnp.max(jnp.abs(blocks), axis=(-3, -1))) + 1e-06
    scaled = (blocks / largest[..., :, None, :, None]).astype(jnp.bfloat16).reshape(full_shape)
    return (scaled, largest)

def slot_table(placement, holders, per_device):
    matches = (placement[:, None, :] == jnp.arange(holders, dtype=jnp.int32)[None, :, None]).astype(jnp.int32)
    rank_within = jnp.cumsum(matches, axis=-1) - 1
    expert_ids = jnp.arange(placement.shape[-1], dtype=jnp.int32)
    slot_numbers = jnp.arange(per_device, dtype=jnp.int32)
    selected = matches[..., None, :] * (rank_within[..., None, :] == slot_numbers[:, None]).astype(jnp.int32)
    return lax.optimization_barrier(jnp.sum(selected * expert_ids, axis=-1)).astype(jnp.int32)

def reference(master, gradient, second, placement):
    values = gradient.astype(jnp.float32)
    square_sum = jnp.sum(values * values)
    root_mean = jnp.sqrt(square_sum / (EXPERTS * FF * D) + 1e-06)
    clipped = values / root_mean
    second_new = decay_rate * second + (1.0 - decay_rate) * clipped * clipped
    master_new = master - step_size * clipped / (jnp.sqrt(second_new) + 1e-08)
    weights = master_new.astype(jnp.bfloat16)
    scaled, largest = block_quantize(weights)
    slot_experts = slot_table(placement, N_EP, EXP_DEV)
    return (master_new, second_new, scaled[slot_experts], largest[slot_experts])
```

```python
import functools

import jax
import jax.numpy as jnp
from jax import lax
from jax.experimental import pallas as pl
from jax.experimental.pallas import tpu as pltpu
from jax.sharding import PartitionSpec as P

BLOCK = 128
HEIGHT = 64
MESH = pl.DeviceIdType.MESH

decay_rate = 0.95
step_size = 0.3


def slot_table(placement, holders, per_device):
    matches = (placement[:, None, :] == jnp.arange(holders, dtype=jnp.int32)[None, :, None]).astype(
        jnp.int32
    )
    rank_within = jnp.cumsum(matches, axis=-1) - 1
    expert_ids = jnp.arange(placement.shape[-1], dtype=jnp.int32)
    slot_numbers = jnp.arange(per_device, dtype=jnp.int32)
    selected = matches[..., None, :] * (rank_within[..., None, :] == slot_numbers[:, None]).astype(
        jnp.int32
    )
    return jnp.sum(selected * expert_ids, axis=-1)


def exchange_kernel(n_rep, n_ep, rounds, table_ref, w_ref, out_ref, *scratch):
    lands = scratch[:rounds]
    stage, own_sem, keep_sem, zrecv, lsend, rsend, xsend, xrecv = scratch[rounds:]
    z = lax.axis_index("ep")
    me = lax.axis_index("replica")
    per, row_count, _ = w_ref.shape
    height = row_count // rounds

    barrier = pltpu.get_barrier_semaphore()
    for step in range(1, n_rep):
        peer = lax.rem(me + step, n_rep)
        pl.semaphore_signal(barrier, inc=1, device_id={"replica": peer}, device_id_type=MESH)

    @pl.when(z > 0)
    def _():
        pl.semaphore_signal(barrier, inc=1, device_id={"ep": z - 1}, device_id_type=MESH)

    @pl.when(z < n_ep - 1)
    def _():
        pl.semaphore_signal(barrier, inc=1, device_id={"ep": z + 1}, device_id_type=MESH)

    def own_copy(t):
        return pltpu.make_async_copy(
            w_ref.at[:, pl.ds(t * height, height), :],
            lands[t].at[pl.ds(per * z, per)],
            own_sem.at[t],
        )

    for t in range(rounds):
        own_copy(t).start()

    lines = jnp.where(z > 0, 1, 0) + jnp.where(z < n_ep - 1, 1, 0)
    pl.semaphore_wait(barrier, n_rep - 1 + lines)

    def line_copy(t, q, to, sems):
        piece = lands[t].at[pl.ds(per * q, per)]
        return pltpu.make_async_remote_copy(
            src_ref=piece,
            dst_ref=piece,
            send_sem=sems.at[t, q],
            recv_sem=zrecv.at[t, q],
            device_id={"ep": to},
            device_id_type=MESH,
        )

    def left(t, q):
        return line_copy(t, q, z - 1, lsend)

    def right(t, q):
        return line_copy(t, q, z + 1, rsend)

    def send_left(t, q):
        @pl.when(z > 0)
        def _():
            left(t, q).start()

    def send_right(t, q):
        @pl.when(z < n_ep - 1)
        def _():
            right(t, q).start()

    def offer(t):
        own_copy(t).wait()
        send_left(t, z)
        send_right(t, z)

    def rows_of(source, t):
        return pl.ds(pl.multiple_of(source * row_count + t * height, height), height)

    def place_copy(t, step):
        return pltpu.make_async_remote_copy(
            src_ref=stage.at[t % 2, step],
            dst_ref=out_ref.at[:, rows_of(me, t), :],
            send_sem=xsend.at[t, step],
            recv_sem=xrecv.at[t, step],
            device_id={"replica": lax.rem(me + step, n_rep)},
            device_id_type=MESH,
        )

    def keep_copy(t):
        return pltpu.make_async_copy(
            stage.at[t % 2, 0], out_ref.at[:, rows_of(me, t), :], keep_sem.at[t]
        )

    def drain(t):
        keep_copy(t).wait()
        for step in range(1, n_rep):
            place_copy(t, step).wait_send()

    offer(0)
    for t in range(rounds):
        if t + 1 < rounds:
            offer(t + 1)
        for d in range(1, n_ep):

            @pl.when(z + d < n_ep)
            def _():
                left(t, z + d).wait_recv()
                send_left(t, z + d)

            @pl.when(z - d >= 0)
            def _():
                right(t, z - d).wait_recv()
                send_right(t, z - d)

        if t >= 2:
            drain(t - 2)
        for step in list(range(1, n_rep)) + [0]:
            dest = lax.rem(me + step, n_rep)
            for k in range(per):
                expert = table_ref[(dest * n_ep + z) * per + k]
                stage[t % 2, step, k] = lands[t][expert]
            if step:
                place_copy(t, step).start()
            else:
                keep_copy(t).start()

    for t in range(max(rounds - 2, 0), rounds):
        drain(t)
    for t in range(rounds):
        for step in range(1, n_rep):
            place_copy(t, step).wait_recv()
        for d in range(n_ep):

            @pl.when(jnp.logical_and(z + d < n_ep, z > 0))
            def _():
                left(t, z + d).wait_send()

            @pl.when(jnp.logical_and(z - d >= 0, z < n_ep - 1))
            def _():
                right(t, z - d).wait_send()


def exchange(table, weights, n_rep, n_ep):
    per, row_count, col_count = weights.shape
    rounds = row_count // HEIGHT
    dma = pltpu.SemaphoreType.DMA
    moved = 2 * per * n_rep * row_count * col_count * 2
    return pl.pallas_call(
        functools.partial(exchange_kernel, n_rep, n_ep, rounds),
        out_shape=jax.ShapeDtypeStruct((per, n_rep * row_count, col_count), weights.dtype),
        in_specs=[
            pl.BlockSpec(memory_space=pltpu.SMEM),
            pl.BlockSpec(memory_space=pl.ANY),
        ],
        out_specs=pl.BlockSpec(memory_space=pl.ANY),
        scratch_shapes=[
            pltpu.VMEM((per * n_ep, HEIGHT, col_count), weights.dtype) for _ in range(rounds)
        ]
        + [
            pltpu.VMEM((2, n_rep, per, HEIGHT, col_count), weights.dtype),
            dma((rounds,)),
            dma((rounds,)),
            dma((rounds, n_ep)),
            dma((rounds, n_ep)),
            dma((rounds, n_ep)),
            dma((rounds, n_rep)),
            dma((rounds, n_rep)),
        ],
        compiler_params=pltpu.CompilerParams(
            collective_id=0, has_side_effects=True, vmem_limit_bytes=52 * 1024 * 1024
        ),
        cost_estimate=pl.CostEstimate(flops=0, bytes_accessed=moved, transcendentals=0),
    )(table, weights)


def scale_kernel(w_ref, out_ref, scale_ref):
    cells = w_ref.shape[2] // BLOCK
    lane = lax.broadcasted_iota(jnp.int32, (1, cells), 1)
    scales = jnp.zeros((1, cells), jnp.float32)
    for cell in range(cells):
        columns = slice(cell * BLOCK, (cell + 1) * BLOCK)
        values = w_ref[0, :, columns].astype(jnp.float32)
        largest = jnp.max(jnp.abs(values), axis=(0, 1), keepdims=True) + 1e-06
        out_ref[0, :, columns] = (values * (1.0 / largest)).astype(out_ref.dtype)
        scales = jnp.where(lane == cell, largest, scales)
    scale_ref[0, 0] = scales


def block_quantize(weights):
    per, row_count, col_count = weights.shape
    strips, cells = row_count // BLOCK, col_count // BLOCK
    scaled, scales = pl.pallas_call(
        scale_kernel,
        grid=(per, strips),
        in_specs=[pl.BlockSpec((1, BLOCK, col_count), lambda k, i: (k, i, 0))],
        out_specs=[
            pl.BlockSpec((1, BLOCK, col_count), lambda k, i: (k, i, 0)),
            pl.BlockSpec((1, 1, 1, cells), lambda k, i: (k, i, 0, 0)),
        ],
        out_shape=[
            jax.ShapeDtypeStruct(weights.shape, weights.dtype),
            jax.ShapeDtypeStruct((per, strips, 1, cells), jnp.float32),
        ],
        compiler_params=pltpu.CompilerParams(vmem_limit_bytes=32 * 1024 * 1024),
    )(weights)
    return scaled, scales[:, :, 0]


def body(master, gradient, second, placement):
    values = gradient.astype(jnp.float32)
    square_sum = lax.psum(jnp.sum(values * values), ("train", "replica", "ep"))
    n_train = lax.axis_size("train")
    n_rep = lax.axis_size("replica")
    n_ep = lax.axis_size("ep")
    root_mean = jnp.sqrt(square_sum / (values.size * n_train * n_rep * n_ep) + 1e-06)
    clipped = values / root_mean
    second_new = decay_rate * second + (1.0 - decay_rate) * clipped * clipped
    master_new = master - step_size * clipped / (jnp.sqrt(second_new) + 1e-08)
    weights = master_new.astype(jnp.bfloat16)
    table = slot_table(placement, n_ep, weights.shape[0]).reshape(-1)
    gathered = exchange(table, weights, n_rep, n_ep)
    scaled, scales = block_quantize(gathered)
    return (master_new, second_new, scaled[None, None], scales[None, None])


def solution(mesh):
    return jax.shard_map(
        body,
        mesh=mesh,
        in_specs=(
            P("ep", "replica", "train"),
            P("ep", "replica", "train"),
            P("ep", "replica", "train"),
            P(),
        ),
        out_specs=(
            P("ep", "replica", "train"),
            P("ep", "replica", "train"),
            P("replica", "ep", None, None, "train"),
            P("replica", "ep", None, None, "train"),
        ),
        check_vma=False,
    )
```

```python
import functools

import jax
import jax.numpy as jnp
from jax import lax
from jax.experimental import pallas as pl
from jax.experimental.pallas import tpu as pltpu
from jax.sharding import PartitionSpec as P

BLOCK = 128
TALL = 64
AHEAD = 2
MESH = pl.DeviceIdType.MESH

decay_rate = 0.95
step_size = 0.3


def slot_table(placement, holders, per_device):
    matches = (placement[:, None, :] == jnp.arange(holders, dtype=jnp.int32)[None, :, None]).astype(
        jnp.int32
    )
    rank_within = jnp.cumsum(matches, axis=-1) - 1
    expert_ids = jnp.arange(placement.shape[-1], dtype=jnp.int32)
    slot_numbers = jnp.arange(per_device, dtype=jnp.int32)
    selected = matches[..., None, :] * (rank_within[..., None, :] == slot_numbers[:, None]).astype(
        jnp.int32
    )
    return jnp.sum(selected * expert_ids, axis=-1)


def route_tables(placement, slots, holders, per_device):
    experts = placement.shape[-1]
    ids = jnp.arange(experts, dtype=jnp.int32)
    needed = jnp.stack(
        [
            jnp.any(placement == 0, axis=0) & (ids >= per_device),
            jnp.any(placement == holders - 1, axis=0) & (ids < experts - per_device),
        ]
    ).astype(jnp.int32)
    rank = jnp.cumsum(needed, axis=-1) - 1
    counts = jnp.sum(needed, axis=-1)
    places = jnp.arange(experts - per_device, dtype=jnp.int32)
    hits = needed[:, None, :] * (rank[:, None, :] == places[None, :, None]).astype(jnp.int32)
    sent = jnp.sum(hits * ids, axis=-1)
    low = jnp.where(ids < per_device, ids, per_device + rank[0])
    high = jnp.where(ids >= experts - per_device, ids, rank[1])
    middle = jnp.broadcast_to(ids, (holders - 2, experts))
    position = jnp.concatenate([low[None], middle, high[None]])
    chosen = (slots[..., None] == ids).astype(jnp.int32)
    read = jnp.sum(chosen * position[None, :, None, :], axis=-1)
    return jnp.concatenate([read.reshape(-1), sent.reshape(-1)]), jnp.max(counts)


def round_heights(rows):
    ramp = [16, 32, 48]
    rest = rows - 2 * sum(ramp)
    if rest >= 0 and rest % TALL == 0:
        return ramp + [TALL] * (rest // TALL) + ramp[::-1]
    return [16] * (rows // 16)


def exchange_kernel(n_rep, n_ep, heights, width, table_ref, w_ref, out_ref, *scratch):
    rounds = len(heights)
    starts = [sum(heights[:t]) for t in range(rounds)]
    lands = scratch[:rounds]
    (stage, packed, own_sem, keep_sem, esend, erecv, zrecv, lsend, rsend, xsend, xrecv) = scratch[
        rounds:
    ]
    z = lax.axis_index("ep")
    me = lax.axis_index("replica")
    per, row_count, _ = w_ref.shape
    goes_left = z >= 2
    goes_right = z <= n_ep - 3
    feeds_end = jnp.logical_or(z == 1, z == n_ep - 2)
    is_end = jnp.logical_or(z == 0, z == n_ep - 1)

    barrier = pltpu.get_barrier_semaphore()
    for step in range(1, n_rep):
        peer = lax.rem(me + step, n_rep)
        pl.semaphore_signal(barrier, inc=1, device_id={"replica": peer}, device_id_type=MESH)

    @pl.when(z > 0)
    def _():
        pl.semaphore_signal(barrier, inc=1, device_id={"ep": z - 1}, device_id_type=MESH)

    @pl.when(z < n_ep - 1)
    def _():
        pl.semaphore_signal(barrier, inc=1, device_id={"ep": z + 1}, device_id_type=MESH)

    def own_copy(t):
        return pltpu.make_async_copy(
            w_ref.at[:, pl.ds(starts[t], heights[t]), :],
            lands[t].at[pl.ds(per * z, per)],
            own_sem.at[t],
        )

    for t in range(rounds):
        own_copy(t).start()

    lines = jnp.where(z > 0, 1, 0) + jnp.where(z < n_ep - 1, 1, 0)
    pl.semaphore_wait(barrier, n_rep - 1 + lines)

    def line_copy(t, q, to, sems):
        piece = lands[t].at[pl.ds(per * q, per)]
        return pltpu.make_async_remote_copy(
            src_ref=piece,
            dst_ref=piece,
            send_sem=sems.at[t, q],
            recv_sem=zrecv.at[t, q],
            device_id={"ep": to},
            device_id_type=MESH,
        )

    def left(t, q):
        return line_copy(t, q, z - 1, lsend)

    def right(t, q):
        return line_copy(t, q, z + 1, rsend)

    def send_left(t, q):
        @pl.when(goes_left)
        def _():
            left(t, q).start()

    def send_right(t, q):
        @pl.when(goes_right)
        def _():
            right(t, q).start()

    def offer(t):
        own_copy(t).wait()
        send_left(t, z)
        send_right(t, z)

    def end_copy(t):
        at_low = z <= 1
        return pltpu.make_async_remote_copy(
            src_ref=packed.at[t % 2, :, pl.ds(0, heights[t]), :],
            dst_ref=lands[t].at[pl.ds(jnp.where(at_low, per, 0), width)],
            send_sem=esend.at[t],
            recv_sem=erecv.at[t],
            device_id={"ep": jnp.where(at_low, 0, n_ep - 1)},
            device_id_type=MESH,
        )

    def rows_of(source, t):
        return pl.ds(pl.multiple_of(source * row_count + starts[t], 16), heights[t])

    def place_copy(t, step):
        return pltpu.make_async_remote_copy(
            src_ref=stage.at[t % 2, step, :, pl.ds(0, heights[t]), :],
            dst_ref=out_ref.at[:, rows_of(me, t), :],
            send_sem=xsend.at[t, step],
            recv_sem=xrecv.at[t, step],
            device_id={"replica": lax.rem(me + step, n_rep)},
            device_id_type=MESH,
        )

    def keep_copy(t):
        return pltpu.make_async_copy(
            stage.at[t % 2, 0, :, pl.ds(0, heights[t]), :],
            out_ref.at[:, rows_of(me, t), :],
            keep_sem.at[t],
        )

    def drain(t):
        keep_copy(t).wait()
        for step in range(1, n_rep):
            place_copy(t, step).wait_send()

    for t in range(min(AHEAD, rounds)):
        offer(t)
    for t in range(rounds):
        if t + AHEAD < rounds:
            offer(t + AHEAD)
        for d in range(1, n_ep):

            @pl.when(jnp.logical_and(z + d < n_ep, z >= 1))
            def _():
                left(t, z + d).wait_recv()
                send_left(t, z + d)

            @pl.when(jnp.logical_and(z - d >= 0, z <= n_ep - 2))
            def _():
                right(t, z - d).wait_recv()
                send_right(t, z - d)

        @pl.when(feeds_end)
        def _():
            if t >= 2:
                end_copy(t - 2).wait_send()
            first = n_rep * n_ep * per + jnp.where(z <= 1, 0, per * (n_ep - 1))
            for i in range(width):
                packed[t % 2, i, : heights[t]] = lands[t][table_ref[first + i]]
            end_copy(t).start()

        @pl.when(is_end)
        def _():
            end_copy(t).wait_recv()

        if t >= 2:
            drain(t - 2)
        for step in list(range(1, n_rep)) + [0]:
            dest = lax.rem(me + step, n_rep)
            for k in range(per):
                slot = table_ref[(dest * n_ep + z) * per + k]
                stage[t % 2, step, k, : heights[t]] = lands[t][slot]
            if step:
                place_copy(t, step).start()
            else:
                keep_copy(t).start()

    for t in range(max(rounds - 2, 0), rounds):
        drain(t)

        @pl.when(feeds_end)
        def _():
            end_copy(t).wait_send()

    for t in range(rounds):
        for step in range(1, n_rep):
            place_copy(t, step).wait_recv()
        for d in range(n_ep):

            @pl.when(jnp.logical_and(z + d < n_ep, goes_left))
            def _():
                left(t, z + d).wait_send()

            @pl.when(jnp.logical_and(z - d >= 0, goes_right))
            def _():
                right(t, z - d).wait_send()


def exchange(table, weights, n_rep, n_ep, width, collective_id):
    per, row_count, col_count = weights.shape
    heights = round_heights(row_count)
    rounds, tallest = len(heights), max(heights)
    dma = pltpu.SemaphoreType.DMA
    moved = 2 * per * n_rep * row_count * col_count * 2
    return pl.pallas_call(
        functools.partial(exchange_kernel, n_rep, n_ep, heights, width),
        out_shape=jax.ShapeDtypeStruct((per, n_rep * row_count, col_count), weights.dtype),
        in_specs=[
            pl.BlockSpec(memory_space=pltpu.SMEM),
            pl.BlockSpec(memory_space=pl.ANY),
        ],
        out_specs=pl.BlockSpec(memory_space=pl.ANY),
        scratch_shapes=[
            pltpu.VMEM((per * n_ep, height, col_count), weights.dtype) for height in heights
        ]
        + [
            pltpu.VMEM((2, n_rep, per, tallest, col_count), weights.dtype),
            pltpu.VMEM((2, width, tallest, col_count), weights.dtype),
            dma((rounds,)),
            dma((rounds,)),
            dma((rounds,)),
            dma((rounds,)),
            dma((rounds, n_ep)),
            dma((rounds, n_ep)),
            dma((rounds, n_ep)),
            dma((rounds, n_rep)),
            dma((rounds, n_rep)),
        ],
        compiler_params=pltpu.CompilerParams(
            collective_id=collective_id, has_side_effects=True, vmem_limit_bytes=54 * 1024 * 1024
        ),
        cost_estimate=pl.CostEstimate(flops=0, bytes_accessed=moved, transcendentals=0),
    )(table, weights)


def total_kernel(axes, x_ref, out_ref, *scratch):
    barrier = pltpu.get_barrier_semaphore()
    for name, size in axes:
        me = lax.axis_index(name)
        for step in range(1, size):
            pl.semaphore_signal(
                barrier,
                inc=1,
                device_id={name: lax.rem(me + step, size)},
                device_id_type=MESH,
            )
    pl.semaphore_wait(barrier, sum(size - 1 for _, size in axes))
    current = x_ref[...]
    for phase, (name, size) in enumerate(axes):
        held, send_sem, recv_sem = scratch[3 * phase : 3 * phase + 3]
        me = lax.axis_index(name)
        held[me] = current
        copies = []
        for step in range(1, size):
            copy = pltpu.make_async_remote_copy(
                src_ref=held.at[me],
                dst_ref=held.at[me],
                send_sem=send_sem.at[step],
                recv_sem=recv_sem.at[step],
                device_id={name: lax.rem(me + step, size)},
                device_id_type=MESH,
            )
            copy.start()
            copies.append(copy)
        for copy in copies:
            copy.wait()
        current = held[0]
        for index in range(1, size):
            current = current + held[index]
    out_ref[...] = current


def total(value, axes, collective_id):
    scratch = []
    for _, size in axes:
        scratch += [
            pltpu.VMEM((size, 8, 128), jnp.float32),
            pltpu.SemaphoreType.DMA((size,)),
            pltpu.SemaphoreType.DMA((size,)),
        ]
    summed = pl.pallas_call(
        functools.partial(total_kernel, axes),
        out_shape=jax.ShapeDtypeStruct((8, 128), jnp.float32),
        in_specs=[pl.BlockSpec(memory_space=pltpu.VMEM)],
        out_specs=pl.BlockSpec(memory_space=pltpu.VMEM),
        scratch_shapes=scratch,
        compiler_params=pltpu.CompilerParams(collective_id=collective_id, has_side_effects=True),
    )(jnp.broadcast_to(value, (8, 128)))
    return summed[0, 0]


def scale_kernel(w_ref, out_ref, scale_ref):
    cells = w_ref.shape[2] // BLOCK
    lane = lax.broadcasted_iota(jnp.int32, (1, cells), 1)
    for strip in range(w_ref.shape[1] // BLOCK):
        rows = slice(strip * BLOCK, (strip + 1) * BLOCK)
        peaks = []
        for cell in range(cells):
            columns = slice(cell * BLOCK, (cell + 1) * BLOCK)
            sizes = jnp.abs(w_ref[0, rows, columns]).reshape(BLOCK // 16, 16, BLOCK)
            column_peaks = jnp.max(jnp.max(sizes, axis=0).astype(jnp.float32), axis=0, keepdims=True)
            peaks.append(jnp.max(column_peaks, axis=1, keepdims=True) + 1e-06)
        scales = jnp.zeros((1, cells), jnp.float32)
        for cell, largest in enumerate(peaks):
            columns = slice(cell * BLOCK, (cell + 1) * BLOCK)
            values = w_ref[0, rows, columns].astype(jnp.float32)
            out_ref[0, rows, columns] = (values * (1.0 / largest)).astype(out_ref.dtype)
            scales = jnp.where(lane == cell, largest, scales)
        scale_ref[0, strip] = scales


def block_quantize(weights):
    per, row_count, col_count = weights.shape
    strips, cells = row_count // BLOCK, col_count // BLOCK
    group = 2 if strips % 2 == 0 else 1
    scaled, scales = pl.pallas_call(
        scale_kernel,
        grid=(per, strips // group),
        in_specs=[pl.BlockSpec((1, group * BLOCK, col_count), lambda k, i: (k, i, 0))],
        out_specs=[
            pl.BlockSpec((1, group * BLOCK, col_count), lambda k, i: (k, i, 0)),
            pl.BlockSpec((1, group, 1, cells), lambda k, i: (k, i, 0, 0)),
        ],
        out_shape=[
            jax.ShapeDtypeStruct(weights.shape, weights.dtype),
            jax.ShapeDtypeStruct((per, strips, 1, cells), jnp.float32),
        ],
        compiler_params=pltpu.CompilerParams(vmem_limit_bytes=32 * 1024 * 1024),
    )(weights)
    return scaled, scales[:, :, 0]


def body(master, gradient, second, placement):
    values = gradient.astype(jnp.float32)
    n_train = lax.axis_size("train")
    n_rep = lax.axis_size("replica")
    n_ep = lax.axis_size("ep")
    axes = (("train", n_train), ("replica", n_rep), ("ep", n_ep))
    square_sum = total(jnp.sum(values * values), axes, 0)
    root_mean = jnp.sqrt(square_sum / (values.size * n_train * n_rep * n_ep) + 1e-06)
    clipped = values / root_mean
    second_new = decay_rate * second + (1.0 - decay_rate) * clipped * clipped
    master_new = master - step_size * clipped / (jnp.sqrt(second_new) + 1e-08)
    weights = master_new.astype(jnp.bfloat16)
    per = weights.shape[0]
    table, most = route_tables(placement, slot_table(placement, n_ep, per), n_ep, per)
    widths = list(range(per * (n_ep - 2), per * (n_ep - 1) + 1))

    def at_width(index, width):
        def run(operands):
            return block_quantize(exchange(*operands, n_rep, n_ep, width, 1 + index))

        return run

    scaled, scales = lax.switch(
        jnp.clip(most - widths[0], 0, len(widths) - 1),
        [at_width(index, width) for index, width in enumerate(widths)],
        (table, weights),
    )
    return (master_new, second_new, scaled[None, None], scales[None, None])


def solution(mesh):
    return jax.shard_map(
        body,
        mesh=mesh,
        in_specs=(
            P("ep", "replica", "train"),
            P("ep", "replica", "train"),
            P("ep", "replica", "train"),
            P(),
        ),
        out_specs=(
            P("ep", "replica", "train"),
            P("ep", "replica", "train"),
            P("replica", "ep", None, None, "train"),
            P("replica", "ep", None, None, "train"),
        ),
        check_vma=False,
    )
```

```python
import functools

import jax
import jax.numpy as jnp
from jax import lax
from jax.experimental import pallas as pl
from jax.experimental.pallas import tpu as pltpu
from jax.sharding import PartitionSpec as P

BLOCK = 128
TALL = 64
AHEAD = 3
DEPTH = 6
MESH = pl.DeviceIdType.MESH

decay_rate = 0.95
step_size = 0.3


def slot_table(placement, holders, per_device):
    matches = (placement[:, None, :] == jnp.arange(holders, dtype=jnp.int32)[None, :, None]).astype(
        jnp.int32
    )
    rank_within = jnp.cumsum(matches, axis=-1) - 1
    expert_ids = jnp.arange(placement.shape[-1], dtype=jnp.int32)
    slot_numbers = jnp.arange(per_device, dtype=jnp.int32)
    selected = matches[..., None, :] * (rank_within[..., None, :] == slot_numbers[:, None]).astype(
        jnp.int32
    )
    return jnp.sum(selected * expert_ids, axis=-1)


def route_tables(placement, slots, holders, per_device):
    experts = placement.shape[-1]
    ids = jnp.arange(experts, dtype=jnp.int32)
    needed = jnp.stack(
        [
            jnp.any(placement == 0, axis=0) & (ids >= per_device),
            jnp.any(placement == holders - 1, axis=0) & (ids < experts - per_device),
        ]
    ).astype(jnp.int32)
    rank = jnp.cumsum(needed, axis=-1) - 1
    counts = jnp.sum(needed, axis=-1)
    places = jnp.arange(experts - per_device, dtype=jnp.int32)
    hits = needed[:, None, :] * (rank[:, None, :] == places[None, :, None]).astype(jnp.int32)
    sent = jnp.sum(hits * ids, axis=-1)
    low = jnp.where(ids < per_device, ids, per_device + rank[0])
    high = jnp.where(ids >= experts - per_device, ids, rank[1])
    middle = jnp.broadcast_to(ids, (holders - 2, experts))
    position = jnp.concatenate([low[None], middle, high[None]])
    chosen = (slots[..., None] == ids).astype(jnp.int32)
    read = jnp.sum(chosen * position[None, :, None, :], axis=-1)
    return jnp.concatenate([read.reshape(-1), sent.reshape(-1)]), jnp.max(counts)


def round_heights(rows):
    ramp = [16, 32, 48]
    rest = rows - 2 * sum(ramp)
    if rest >= 0 and rest % TALL == 0:
        return ramp + [TALL] * (rest // TALL) + ramp[::-1]
    return [16] * (rows // 16)


def exchange_kernel(n_rep, n_ep, heights, width, table_ref, w_ref, out_ref, *scratch):
    rounds = len(heights)
    starts = [sum(heights[:t]) for t in range(rounds)]
    lands = scratch[:rounds]
    (stage, packed, own_sem, keep_sem, esend, erecv, zrecv, lsend, rsend, xsend, xrecv) = scratch[
        rounds:
    ]
    z = lax.axis_index("ep")
    me = lax.axis_index("replica")
    per, row_count, _ = w_ref.shape
    goes_left = z >= 2
    goes_right = z <= n_ep - 3
    feeds_end = jnp.logical_or(z == 1, z == n_ep - 2)
    is_end = jnp.logical_or(z == 0, z == n_ep - 1)

    barrier = pltpu.get_barrier_semaphore()
    for step in range(1, n_rep):
        peer = lax.rem(me + step, n_rep)
        pl.semaphore_signal(barrier, inc=1, device_id={"replica": peer}, device_id_type=MESH)

    @pl.when(z > 0)
    def _():
        pl.semaphore_signal(barrier, inc=1, device_id={"ep": z - 1}, device_id_type=MESH)

    @pl.when(z < n_ep - 1)
    def _():
        pl.semaphore_signal(barrier, inc=1, device_id={"ep": z + 1}, device_id_type=MESH)

    def own_copy(t):
        return pltpu.make_async_copy(
            w_ref.at[:, pl.ds(starts[t], heights[t]), :],
            lands[t].at[pl.ds(per * z, per)],
            own_sem.at[t],
        )

    for t in range(rounds):
        own_copy(t).start()

    lines = jnp.where(z > 0, 1, 0) + jnp.where(z < n_ep - 1, 1, 0)
    pl.semaphore_wait(barrier, n_rep - 1 + lines)

    def line_copy(t, q, to, sems):
        piece = lands[t].at[pl.ds(per * q, per)]
        return pltpu.make_async_remote_copy(
            src_ref=piece,
            dst_ref=piece,
            send_sem=sems.at[t, q],
            recv_sem=zrecv.at[t, q],
            device_id={"ep": to},
            device_id_type=MESH,
        )

    def left(t, q):
        return line_copy(t, q, z - 1, lsend)

    def right(t, q):
        return line_copy(t, q, z + 1, rsend)

    def send_left(t, q):
        @pl.when(goes_left)
        def _():
            left(t, q).start()

    def send_right(t, q):
        @pl.when(goes_right)
        def _():
            right(t, q).start()

    def offer(t):
        own_copy(t).wait()
        send_left(t, z)
        send_right(t, z)

    def end_copy(t):
        at_low = z <= 1
        return pltpu.make_async_remote_copy(
            src_ref=packed.at[t % 2, :, pl.ds(0, heights[t]), :],
            dst_ref=lands[t].at[pl.ds(jnp.where(at_low, per, 0), width)],
            send_sem=esend.at[t],
            recv_sem=erecv.at[t],
            device_id={"ep": jnp.where(at_low, 0, n_ep - 1)},
            device_id_type=MESH,
        )

    def rows_of(source, t):
        return pl.ds(pl.multiple_of(source * row_count + starts[t], 16), heights[t])

    def place_copy(t, step):
        return pltpu.make_async_remote_copy(
            src_ref=stage.at[t % 2, step, :, pl.ds(0, heights[t]), :],
            dst_ref=out_ref.at[:, rows_of(me, t), :],
            send_sem=xsend.at[t, step],
            recv_sem=xrecv.at[t, step],
            device_id={"replica": lax.rem(me + step, n_rep)},
            device_id_type=MESH,
        )

    def keep_copy(t):
        return pltpu.make_async_copy(
            stage.at[t % 2, 0, :, pl.ds(0, heights[t]), :],
            out_ref.at[:, rows_of(me, t), :],
            keep_sem.at[t],
        )

    def drain(t):
        keep_copy(t).wait()
        for step in range(1, n_rep):
            place_copy(t, step).wait_send()

    def offer_if(wanted, t):
        if t < rounds:

            @pl.when(wanted)
            def _():
                offer(t)

    def relay(t):
        for d in range(1, n_ep):

            @pl.when(jnp.logical_and(z + d < n_ep, goes_left))
            def _():
                left(t, z + d).wait_recv()
                send_left(t, z + d)

            @pl.when(jnp.logical_and(z - d >= 0, goes_right))
            def _():
                right(t, z - d).wait_recv()
                send_right(t, z - d)

    def arrive(t):
        for d in range(1, n_ep):

            @pl.when(jnp.logical_and(z + d < n_ep, z == 1))
            def _():
                left(t, z + d).wait_recv()

            @pl.when(jnp.logical_and(z - d >= 0, z == n_ep - 2))
            def _():
                right(t, z - d).wait_recv()

    within = jnp.logical_not(is_end)
    for t in range(AHEAD):
        offer_if(is_end, t)
    offer_if(is_end, AHEAD)
    offer_if(within, 0)
    relay(0)
    offer_if(within, 1)
    for t in range(rounds):
        if t + 1 < rounds:
            relay(t + 1)
        offer_if(within, t + 2)
        offer_if(is_end, t + AHEAD + 1)
        arrive(t)

        @pl.when(feeds_end)
        def _():
            if t >= 2:
                end_copy(t - 2).wait_send()
            first = n_rep * n_ep * per + jnp.where(z <= 1, 0, per * (n_ep - 1))
            for i in range(width):
                packed[t % 2, i, : heights[t]] = lands[t][table_ref[first + i]]
            end_copy(t).start()

        @pl.when(is_end)
        def _():
            end_copy(t).wait_recv()

        if t >= 2:
            drain(t - 2)
        for step in list(range(1, n_rep)) + [0]:
            dest = lax.rem(me + step, n_rep)
            for k in range(per):
                slot = table_ref[(dest * n_ep + z) * per + k]
                stage[t % 2, step, k, : heights[t]] = lands[t][slot]
            if step:
                place_copy(t, step).start()
            else:
                keep_copy(t).start()

    for t in range(max(rounds - 2, 0), rounds):
        drain(t)

        @pl.when(feeds_end)
        def _():
            end_copy(t).wait_send()

    for t in range(rounds):
        for step in range(1, n_rep):
            place_copy(t, step).wait_recv()
        for d in range(n_ep):

            @pl.when(jnp.logical_and(z + d < n_ep, goes_left))
            def _():
                left(t, z + d).wait_send()

            @pl.when(jnp.logical_and(z - d >= 0, goes_right))
            def _():
                right(t, z - d).wait_send()


def exchange(table, weights, n_rep, n_ep, width, collective_id):
    per, row_count, col_count = weights.shape
    heights = round_heights(row_count)
    rounds, tallest = len(heights), max(heights)
    dma = pltpu.SemaphoreType.DMA
    moved = 2 * per * n_rep * row_count * col_count * 2
    return pl.pallas_call(
        functools.partial(exchange_kernel, n_rep, n_ep, heights, width),
        out_shape=jax.ShapeDtypeStruct((per, n_rep * row_count, col_count), weights.dtype),
        in_specs=[
            pl.BlockSpec(memory_space=pltpu.SMEM),
            pl.BlockSpec(memory_space=pl.ANY),
        ],
        out_specs=pl.BlockSpec(memory_space=pl.ANY),
        scratch_shapes=[
            pltpu.VMEM((per * n_ep, height, col_count), weights.dtype) for height in heights
        ]
        + [
            pltpu.VMEM((2, n_rep, per, tallest, col_count), weights.dtype),
            pltpu.VMEM((2, width, tallest, col_count), weights.dtype),
            dma((rounds,)),
            dma((rounds,)),
            dma((rounds,)),
            dma((rounds,)),
            dma((rounds, n_ep)),
            dma((rounds, n_ep)),
            dma((rounds, n_ep)),
            dma((rounds, n_rep)),
            dma((rounds, n_rep)),
        ],
        compiler_params=pltpu.CompilerParams(
            collective_id=collective_id, has_side_effects=True, vmem_limit_bytes=54 * 1024 * 1024
        ),
        cost_estimate=pl.CostEstimate(flops=0, bytes_accessed=moved, transcendentals=0),
    )(table, weights)


def total_kernel(axes, x_ref, out_ref, *scratch):
    barrier = pltpu.get_barrier_semaphore()
    for name, size in axes:
        me = lax.axis_index(name)
        for step in range(1, size):
            pl.semaphore_signal(
                barrier,
                inc=1,
                device_id={name: lax.rem(me + step, size)},
                device_id_type=MESH,
            )
    pl.semaphore_wait(barrier, sum(size - 1 for _, size in axes))
    current = x_ref[...]
    for phase, (name, size) in enumerate(axes):
        held, send_sem, recv_sem = scratch[3 * phase : 3 * phase + 3]
        me = lax.axis_index(name)
        held[me] = current
        copies = []
        for step in range(1, size):
            copy = pltpu.make_async_remote_copy(
                src_ref=held.at[me],
                dst_ref=held.at[me],
                send_sem=send_sem.at[step],
                recv_sem=recv_sem.at[step],
                device_id={name: lax.rem(me + step, size)},
                device_id_type=MESH,
            )
            copy.start()
            copies.append(copy)
        for copy in copies:
            copy.wait()
        current = held[0]
        for index in range(1, size):
            current = current + held[index]
    out_ref[...] = current


def total(value, axes, collective_id):
    scratch = []
    for _, size in axes:
        scratch += [
            pltpu.VMEM((size, 8, 128), jnp.float32),
            pltpu.SemaphoreType.DMA((size,)),
            pltpu.SemaphoreType.DMA((size,)),
        ]
    summed = pl.pallas_call(
        functools.partial(total_kernel, axes),
        out_shape=jax.ShapeDtypeStruct((8, 128), jnp.float32),
        in_specs=[pl.BlockSpec(memory_space=pltpu.VMEM)],
        out_specs=pl.BlockSpec(memory_space=pltpu.VMEM),
        scratch_shapes=scratch,
        compiler_params=pltpu.CompilerParams(collective_id=collective_id, has_side_effects=True),
    )(jnp.broadcast_to(value, (8, 128)))
    return summed[0, 0]


def scale_kernel(w_ref, out_ref, scale_ref, held, made, in_sem, out_sem):
    count, _, col_count = w_ref.shape
    cells = col_count // BLOCK
    depth = held.shape[0]
    lane = lax.broadcasted_iota(jnp.int32, (1, cells), 1)

    def fetch(strip):
        slot = lax.rem(strip, depth)
        return pltpu.make_async_copy(w_ref.at[strip], held.at[slot], in_sem.at[slot])

    def put(strip):
        slot = lax.rem(strip, depth)
        return pltpu.make_async_copy(made.at[slot], out_ref.at[strip], out_sem.at[slot])

    def start(strip, carry):
        fetch(strip).start()
        return carry

    def work(strip, carry):
        slot = lax.rem(strip, depth)
        fetch(strip).wait()

        @pl.when(strip >= depth)
        def _():
            put(strip - depth).wait()

        peaks = []
        for cell in range(cells):
            columns = slice(cell * BLOCK, (cell + 1) * BLOCK)
            sizes = jnp.abs(held[slot, :, columns]).reshape(BLOCK // 16, 16, BLOCK)
            column_peaks = jnp.max(jnp.max(sizes, axis=0).astype(jnp.float32), axis=0, keepdims=True)
            peaks.append(jnp.max(column_peaks, axis=1, keepdims=True) + 1e-06)
        scales = jnp.zeros((1, cells), jnp.float32)
        for cell, largest in enumerate(peaks):
            columns = slice(cell * BLOCK, (cell + 1) * BLOCK)
            values = held[slot, :, columns].astype(jnp.float32)
            made[slot, :, columns] = (values * (1.0 / largest)).astype(made.dtype)
            scales = jnp.where(lane == cell, largest, scales)
        scale_ref[strip] = scales
        put(strip).start()

        @pl.when(strip + depth < count)
        def _():
            fetch(strip + depth).start()

        return carry

    def finish(strip, carry):
        put(strip).wait()
        return carry

    lax.fori_loop(0, depth, start, 0)
    lax.fori_loop(0, count, work, 0)
    lax.fori_loop(count - depth, count, finish, 0)


def block_quantize(weights):
    per, row_count, col_count = weights.shape
    strips, cells = row_count // BLOCK, col_count // BLOCK
    count = per * strips
    depth = min(DEPTH, count)
    scaled, scales = pl.pallas_call(
        scale_kernel,
        in_specs=[pl.BlockSpec(memory_space=pl.ANY)],
        out_specs=[
            pl.BlockSpec(memory_space=pl.ANY),
            pl.BlockSpec(memory_space=pltpu.VMEM),
        ],
        out_shape=[
            jax.ShapeDtypeStruct((count, BLOCK, col_count), weights.dtype),
            jax.ShapeDtypeStruct((count, 1, cells), jnp.float32),
        ],
        scratch_shapes=[
            pltpu.VMEM((depth, BLOCK, col_count), weights.dtype),
            pltpu.VMEM((depth, BLOCK, col_count), weights.dtype),
            pltpu.SemaphoreType.DMA((depth,)),
            pltpu.SemaphoreType.DMA((depth,)),
        ],
        compiler_params=pltpu.CompilerParams(vmem_limit_bytes=32 * 1024 * 1024),
    )(weights.reshape(count, BLOCK, col_count))
    return scaled.reshape(weights.shape), scales.reshape(per, strips, cells)


def body(master, gradient, second, placement):
    values = gradient.astype(jnp.float32)
    n_train = lax.axis_size("train")
    n_rep = lax.axis_size("replica")
    n_ep = lax.axis_size("ep")
    axes = (("train", n_train), ("replica", n_rep), ("ep", n_ep))
    square_sum = total(jnp.sum(values * values), axes, 0)
    root_mean = jnp.sqrt(square_sum / (values.size * n_train * n_rep * n_ep) + 1e-06)
    clipped = values / root_mean
    second_new = decay_rate * second + (1.0 - decay_rate) * clipped * clipped
    master_new = master - step_size * clipped / (jnp.sqrt(second_new) + 1e-08)
    weights = master_new.astype(jnp.bfloat16)
    per = weights.shape[0]
    table, most = route_tables(placement, slot_table(placement, n_ep, per), n_ep, per)
    widths = list(range(per * (n_ep - 2), per * (n_ep - 1) + 1))

    def at_width(index, width):
        def run(operands):
            return block_quantize(exchange(*operands, n_rep, n_ep, width, 1 + index))

        return run

    scaled, scales = lax.switch(
        jnp.clip(most - widths[0], 0, len(widths) - 1),
        [at_width(index, width) for index, width in enumerate(widths)],
        (table, weights),
    )
    return (master_new, second_new, scaled[None, None], scales[None, None])


def solution(mesh):
    return jax.shard_map(
        body,
        mesh=mesh,
        in_specs=(
            P("ep", "replica", "train"),
            P("ep", "replica", "train"),
            P("ep", "replica", "train"),
            P(),
        ),
        out_specs=(
            P("ep", "replica", "train"),
            P("ep", "replica", "train"),
            P("replica", "ep", None, None, "train"),
            P("replica", "ep", None, None, "train"),
        ),
        check_vma=False,
    )
```

```python
import functools

import jax
import jax.numpy as jnp
from jax import lax
from jax.experimental import pallas as pl
from jax.experimental.pallas import tpu as pltpu
from jax.sharding import PartitionSpec as P

BLOCK = 128
TALL = 32
RING = 4
AHEAD = 3
DEPTH = 6
MESH = pl.DeviceIdType.MESH

decay_rate = 0.95
step_size = 0.3


def slot_table(placement, holders, per_device):
    matches = (placement[:, None, :] == jnp.arange(holders, dtype=jnp.int32)[None, :, None]).astype(
        jnp.int32
    )
    rank_within = jnp.cumsum(matches, axis=-1) - 1
    expert_ids = jnp.arange(placement.shape[-1], dtype=jnp.int32)
    slot_numbers = jnp.arange(per_device, dtype=jnp.int32)
    selected = matches[..., None, :] * (rank_within[..., None, :] == slot_numbers[:, None]).astype(
        jnp.int32
    )
    return jnp.sum(selected * expert_ids, axis=-1)


def route_tables(placement, slots, holders, per_device):
    experts = placement.shape[-1]
    ids = jnp.arange(experts, dtype=jnp.int32)
    needed = jnp.stack(
        [
            jnp.any(placement == 0, axis=0) & (ids >= per_device),
            jnp.any(placement == holders - 1, axis=0) & (ids < experts - per_device),
        ]
    ).astype(jnp.int32)
    rank = jnp.cumsum(needed, axis=-1) - 1
    counts = jnp.sum(needed, axis=-1)
    places = jnp.arange(experts - per_device, dtype=jnp.int32)
    hits = needed[:, None, :] * (rank[:, None, :] == places[None, :, None]).astype(jnp.int32)
    sent = jnp.sum(hits * ids, axis=-1)
    low = jnp.where(ids < per_device, ids, per_device + rank[0])
    high = jnp.where(ids >= experts - per_device, ids, rank[1])
    middle = jnp.broadcast_to(ids, (holders - 2, experts))
    position = jnp.concatenate([low[None], middle, high[None]])
    chosen = (slots[..., None] == ids).astype(jnp.int32)
    read = jnp.sum(chosen * position[None, :, None, :], axis=-1)
    return jnp.concatenate([read.reshape(-1), sent.reshape(-1)]), jnp.max(counts)


def round_heights(rows):
    ramp = [16]
    rest = rows - 2 * sum(ramp)
    if rest >= 0 and rest % TALL == 0:
        return ramp + [TALL] * (rest // TALL) + ramp[::-1]
    return [16] * (rows // 16)


def exchange_kernel(n_rep, n_ep, heights, width, table_ref, w_ref, out_ref, *scratch):
    rounds = len(heights)
    starts = [sum(heights[:t]) for t in range(rounds)]
    lands = scratch[:rounds]
    (stage, packed, own_sem, keep_sem, esend, erecv, zrecv, lsend, rsend, xsend, xrecv) = scratch[
        rounds:
    ]
    z = lax.axis_index("ep")
    me = lax.axis_index("replica")
    per, row_count, _ = w_ref.shape
    goes_left = z >= 2
    goes_right = z <= n_ep - 3
    feeds_end = jnp.logical_or(z == 1, z == n_ep - 2)
    is_end = jnp.logical_or(z == 0, z == n_ep - 1)

    barrier = pltpu.get_barrier_semaphore()
    for step in range(1, n_rep):
        peer = lax.rem(me + step, n_rep)
        pl.semaphore_signal(barrier, inc=1, device_id={"replica": peer}, device_id_type=MESH)

    @pl.when(z > 0)
    def _():
        pl.semaphore_signal(barrier, inc=1, device_id={"ep": z - 1}, device_id_type=MESH)

    @pl.when(z < n_ep - 1)
    def _():
        pl.semaphore_signal(barrier, inc=1, device_id={"ep": z + 1}, device_id_type=MESH)

    def own_copy(t):
        return pltpu.make_async_copy(
            w_ref.at[:, pl.ds(starts[t], heights[t]), :],
            lands[t].at[pl.ds(per * z, per)],
            own_sem.at[t],
        )

    for t in range(rounds):
        own_copy(t).start()

    lines = jnp.where(z > 0, 1, 0) + jnp.where(z < n_ep - 1, 1, 0)
    pl.semaphore_wait(barrier, n_rep - 1 + lines)

    def line_copy(t, q, to, sems):
        piece = lands[t].at[pl.ds(per * q, per)]
        return pltpu.make_async_remote_copy(
            src_ref=piece,
            dst_ref=piece,
            send_sem=sems.at[t, q],
            recv_sem=zrecv.at[t, q],
            device_id={"ep": to},
            device_id_type=MESH,
        )

    def left(t, q):
        return line_copy(t, q, z - 1, lsend)

    def right(t, q):
        return line_copy(t, q, z + 1, rsend)

    def send_left(t, q):
        @pl.when(goes_left)
        def _():
            left(t, q).start()

    def send_right(t, q):
        @pl.when(goes_right)
        def _():
            right(t, q).start()

    def offer(t):
        own_copy(t).wait()
        send_left(t, z)
        send_right(t, z)

    def end_copy(t):
        at_low = z <= 1
        return pltpu.make_async_remote_copy(
            src_ref=packed.at[t % RING, :, pl.ds(0, heights[t]), :],
            dst_ref=lands[t].at[pl.ds(jnp.where(at_low, per, 0), width)],
            send_sem=esend.at[t],
            recv_sem=erecv.at[t],
            device_id={"ep": jnp.where(at_low, 0, n_ep - 1)},
            device_id_type=MESH,
        )

    def rows_of(source, t):
        return pl.ds(pl.multiple_of(source * row_count + starts[t], 16), heights[t])

    def place_copy(t, step):
        return pltpu.make_async_remote_copy(
            src_ref=stage.at[t % RING, step, :, pl.ds(0, heights[t]), :],
            dst_ref=out_ref.at[:, rows_of(me, t), :],
            send_sem=xsend.at[t, step],
            recv_sem=xrecv.at[t, step],
            device_id={"replica": lax.rem(me + step, n_rep)},
            device_id_type=MESH,
        )

    def keep_copy(t):
        return pltpu.make_async_copy(
            stage.at[t % RING, 0, :, pl.ds(0, heights[t]), :],
            out_ref.at[:, rows_of(me, t), :],
            keep_sem.at[t],
        )

    def drain(t):
        keep_copy(t).wait()
        for step in range(1, n_rep):
            place_copy(t, step).wait_send()

    def offer_if(wanted, t):
        if t < rounds:

            @pl.when(wanted)
            def _():
                offer(t)

    def relay(t):
        for d in range(1, n_ep):

            @pl.when(jnp.logical_and(z + d < n_ep, goes_left))
            def _():
                left(t, z + d).wait_recv()
                send_left(t, z + d)

            @pl.when(jnp.logical_and(z - d >= 0, goes_right))
            def _():
                right(t, z - d).wait_recv()
                send_right(t, z - d)

    def arrive(t):
        for d in range(1, n_ep):

            @pl.when(jnp.logical_and(z + d < n_ep, z == 1))
            def _():
                left(t, z + d).wait_recv()

            @pl.when(jnp.logical_and(z - d >= 0, z == n_ep - 2))
            def _():
                right(t, z - d).wait_recv()

    within = jnp.logical_not(is_end)
    for t in range(AHEAD):
        offer_if(is_end, t)
    offer_if(is_end, AHEAD)
    offer_if(within, 0)
    relay(0)
    offer_if(within, 1)
    for t in range(rounds):
        if t + 1 < rounds:
            relay(t + 1)
        offer_if(within, t + 2)
        offer_if(is_end, t + AHEAD + 1)
        arrive(t)

        @pl.when(feeds_end)
        def _():
            if t >= RING:
                end_copy(t - RING).wait_send()
            first = n_rep * n_ep * per + jnp.where(z <= 1, 0, per * (n_ep - 1))
            for i in range(width):
                packed[t % RING, i, : heights[t]] = lands[t][table_ref[first + i]]
            end_copy(t).start()

        @pl.when(is_end)
        def _():
            end_copy(t).wait_recv()

        if t >= RING:
            drain(t - RING)
        for step in list(range(1, n_rep)) + [0]:
            dest = lax.rem(me + step, n_rep)
            for k in range(per):
                slot = table_ref[(dest * n_ep + z) * per + k]
                stage[t % RING, step, k, : heights[t]] = lands[t][slot]
            if step:
                place_copy(t, step).start()
            else:
                keep_copy(t).start()

    for t in range(max(rounds - RING, 0), rounds):
        drain(t)

        @pl.when(feeds_end)
        def _():
            end_copy(t).wait_send()

    for t in range(rounds):
        for step in range(1, n_rep):
            place_copy(t, step).wait_recv()
        for d in range(n_ep):

            @pl.when(jnp.logical_and(z + d < n_ep, goes_left))
            def _():
                left(t, z + d).wait_send()

            @pl.when(jnp.logical_and(z - d >= 0, goes_right))
            def _():
                right(t, z - d).wait_send()


def exchange(table, weights, n_rep, n_ep, width, collective_id):
    per, row_count, col_count = weights.shape
    heights = round_heights(row_count)
    rounds, tallest = len(heights), max(heights)
    dma = pltpu.SemaphoreType.DMA
    moved = 2 * per * n_rep * row_count * col_count * 2
    return pl.pallas_call(
        functools.partial(exchange_kernel, n_rep, n_ep, heights, width),
        out_shape=jax.ShapeDtypeStruct((per, n_rep * row_count, col_count), weights.dtype),
        in_specs=[
            pl.BlockSpec(memory_space=pltpu.SMEM),
            pl.BlockSpec(memory_space=pl.ANY),
        ],
        out_specs=pl.BlockSpec(memory_space=pl.ANY),
        scratch_shapes=[
            pltpu.VMEM((per * n_ep, height, col_count), weights.dtype) for height in heights
        ]
        + [
            pltpu.VMEM((RING, n_rep, per, tallest, col_count), weights.dtype),
            pltpu.VMEM((RING, width, tallest, col_count), weights.dtype),
            dma((rounds,)),
            dma((rounds,)),
            dma((rounds,)),
            dma((rounds,)),
            dma((rounds, n_ep)),
            dma((rounds, n_ep)),
            dma((rounds, n_ep)),
            dma((rounds, n_rep)),
            dma((rounds, n_rep)),
        ],
        compiler_params=pltpu.CompilerParams(
            collective_id=collective_id, has_side_effects=True, vmem_limit_bytes=54 * 1024 * 1024
        ),
        cost_estimate=pl.CostEstimate(flops=0, bytes_accessed=moved, transcendentals=0),
    )(table, weights)


def total_kernel(axes, x_ref, out_ref, *scratch):
    barrier = pltpu.get_barrier_semaphore()
    for name, size in axes:
        me = lax.axis_index(name)
        for step in range(1, size):
            pl.semaphore_signal(
                barrier,
                inc=1,
                device_id={name: lax.rem(me + step, size)},
                device_id_type=MESH,
            )
    pl.semaphore_wait(barrier, sum(size - 1 for _, size in axes))
    current = x_ref[...]
    for phase, (name, size) in enumerate(axes):
        held, send_sem, recv_sem = scratch[3 * phase : 3 * phase + 3]
        me = lax.axis_index(name)
        held[me] = current
        copies = []
        for step in range(1, size):
            copy = pltpu.make_async_remote_copy(
                src_ref=held.at[me],
                dst_ref=held.at[me],
                send_sem=send_sem.at[step],
                recv_sem=recv_sem.at[step],
                device_id={name: lax.rem(me + step, size)},
                device_id_type=MESH,
            )
            copy.start()
            copies.append(copy)
        for copy in copies:
            copy.wait()
        current = held[0]
        for index in range(1, size):
            current = current + held[index]
    out_ref[...] = current


def total(value, axes, collective_id):
    scratch = []
    for _, size in axes:
        scratch += [
            pltpu.VMEM((size, 8, 128), jnp.float32),
            pltpu.SemaphoreType.DMA((size,)),
            pltpu.SemaphoreType.DMA((size,)),
        ]
    summed = pl.pallas_call(
        functools.partial(total_kernel, axes),
        out_shape=jax.ShapeDtypeStruct((8, 128), jnp.float32),
        in_specs=[pl.BlockSpec(memory_space=pltpu.VMEM)],
        out_specs=pl.BlockSpec(memory_space=pltpu.VMEM),
        scratch_shapes=scratch,
        compiler_params=pltpu.CompilerParams(collective_id=collective_id, has_side_effects=True),
    )(jnp.broadcast_to(value, (8, 128)))
    return summed[0, 0]


def scale_kernel(w_ref, out_ref, scale_ref, held, made, in_sem, out_sem):
    count, _, col_count = w_ref.shape
    cells = col_count // BLOCK
    depth = held.shape[0]
    lane = lax.broadcasted_iota(jnp.int32, (1, cells), 1)

    def fetch(strip):
        slot = lax.rem(strip, depth)
        return pltpu.make_async_copy(w_ref.at[strip], held.at[slot], in_sem.at[slot])

    def put(strip):
        slot = lax.rem(strip, depth)
        return pltpu.make_async_copy(made.at[slot], out_ref.at[strip], out_sem.at[slot])

    def start(strip, carry):
        fetch(strip).start()
        return carry

    def work(strip, carry):
        slot = lax.rem(strip, depth)
        fetch(strip).wait()

        @pl.when(strip >= depth)
        def _():
            put(strip - depth).wait()

        peaks = []
        for cell in range(cells):
            columns = slice(cell * BLOCK, (cell + 1) * BLOCK)
            sizes = jnp.abs(held[slot, :, columns]).reshape(BLOCK // 16, 16, BLOCK)
            column_peaks = jnp.max(jnp.max(sizes, axis=0).astype(jnp.float32), axis=0, keepdims=True)
            peaks.append(jnp.max(column_peaks, axis=1, keepdims=True) + 1e-06)
        scales = jnp.zeros((1, cells), jnp.float32)
        for cell, largest in enumerate(peaks):
            columns = slice(cell * BLOCK, (cell + 1) * BLOCK)
            values = held[slot, :, columns].astype(jnp.float32)
            made[slot, :, columns] = (values * (1.0 / largest)).astype(made.dtype)
            scales = jnp.where(lane == cell, largest, scales)
        scale_ref[strip] = scales
        put(strip).start()

        @pl.when(strip + depth < count)
        def _():
            fetch(strip + depth).start()

        return carry

    def finish(strip, carry):
        put(strip).wait()
        return carry

    lax.fori_loop(0, depth, start, 0)
    lax.fori_loop(0, count, work, 0)
    lax.fori_loop(count - depth, count, finish, 0)


def block_quantize(weights):
    per, row_count, col_count = weights.shape
    strips, cells = row_count // BLOCK, col_count // BLOCK
    count = per * strips
    depth = min(DEPTH, count)
    scaled, scales = pl.pallas_call(
        scale_kernel,
        in_specs=[pl.BlockSpec(memory_space=pl.ANY)],
        out_specs=[
            pl.BlockSpec(memory_space=pl.ANY),
            pl.BlockSpec(memory_space=pltpu.VMEM),
        ],
        out_shape=[
            jax.ShapeDtypeStruct((count, BLOCK, col_count), weights.dtype),
            jax.ShapeDtypeStruct((count, 1, cells), jnp.float32),
        ],
        scratch_shapes=[
            pltpu.VMEM((depth, BLOCK, col_count), weights.dtype),
            pltpu.VMEM((depth, BLOCK, col_count), weights.dtype),
            pltpu.SemaphoreType.DMA((depth,)),
            pltpu.SemaphoreType.DMA((depth,)),
        ],
        compiler_params=pltpu.CompilerParams(vmem_limit_bytes=32 * 1024 * 1024),
    )(weights.reshape(count, BLOCK, col_count))
    return scaled.reshape(weights.shape), scales.reshape(per, strips, cells)


def body(master, gradient, second, placement):
    values = gradient.astype(jnp.float32)
    n_train = lax.axis_size("train")
    n_rep = lax.axis_size("replica")
    n_ep = lax.axis_size("ep")
    axes = (("train", n_train), ("replica", n_rep), ("ep", n_ep))
    square_sum = total(jnp.sum(values * values), axes, 0)
    root_mean = jnp.sqrt(square_sum / (values.size * n_train * n_rep * n_ep) + 1e-06)
    clipped = values / root_mean
    second_new = decay_rate * second + (1.0 - decay_rate) * clipped * clipped
    master_new = master - step_size * clipped / (jnp.sqrt(second_new) + 1e-08)
    weights = master_new.astype(jnp.bfloat16)
    per = weights.shape[0]
    table, most = route_tables(placement, slot_table(placement, n_ep, per), n_ep, per)
    widths = list(range(per * (n_ep - 2), per * (n_ep - 1) + 1))

    def at_width(index, width):
        def run(operands):
            return block_quantize(exchange(*operands, n_rep, n_ep, width, 1 + index))

        return run

    scaled, scales = lax.switch(
        jnp.clip(most - widths[0], 0, len(widths) - 1),
        [at_width(index, width) for index, width in enumerate(widths)],
        (table, weights),
    )
    return (master_new, second_new, scaled[None, None], scales[None, None])


def solution(mesh):
    return jax.shard_map(
        body,
        mesh=mesh,
        in_specs=(
            P("ep", "replica", "train"),
            P("ep", "replica", "train"),
            P("ep", "replica", "train"),
            P(),
        ),
        out_specs=(
            P("ep", "replica", "train"),
            P("ep", "replica", "train"),
            P("replica", "ep", None, None, "train"),
            P("replica", "ep", None, None, "train"),
        ),
        check_vma=False,
    )
```
